32 devices in a mesh: groups: 2 (over x), rows: 16 (over z, y, core).
Axes of the slice: x: 2, y: 2, z: 4, core: 2. Of those that a mesh axis runs over, the one named last changes fastest.
Arguments:
- tiles: bfloat16 [1024, 256, 256], P(('groups', 'rows')), parts along dimension 0, may hold values from -0.375 to 0.375
- tile_rows: int32 [1024], P(('groups', 'rows')), parts along dimension 0, may hold values from 0 to 3
- tile_cols: int32 [1024], P(('groups', 'rows')), parts along dimension 0, may hold values from 0 to 95, as said below
- tile_count: int32 [32], P(('groups', 'rows')), parts along dimension 0, may hold values from 16 to 32, as said below
- right_side: float32 [128, 256], P(('groups', 'rows')), parts along dimension 0, may hold values from -16 to 16
- row_kind: int32 [128, 256], P(('groups', 'rows')), parts along dimension 0, may hold values 0 or 1
- cost: float32 [192, 256], P(('groups', 'rows')), parts along dimension 0, may hold values from -16 to 16
- upper: float32 [192, 256], P(('groups', 'rows')), parts along dimension 0, may hold values from 0.05 to 2
- primal_init: float32 [192, 256], P(('groups', 'rows')), parts along dimension 0, may hold values from 0 to 1
- dual_init: float32 [128, 256], P(('groups', 'rows')), parts along dimension 0, may hold values from -3 to 3
Outputs:
- primal: float32 [192, 256], P(('groups', 'rows')), parts along dimension 0
- dual: float32 [128, 256], P(('groups', 'rows')), parts along dimension 0
- norms: float32 [4, 2], P('groups'), parts along dimension 0
The draws below stay inside these ranges and needn't reach their ends.
There are 2 independent parts, one for each index of `groups`. The reference program is written for one: setup_inputs(seed, part) draws one part's arguments, and reference() takes and returns one part's arrays. A program takes and returns all parts, laid end to end along the dimension named above; each array names one. Nothing has to cross between parts.
Inputs may be any that keep to these rules, and one draw needn't show every extreme that they name: `tile_count`: some device-block has all 32 tiles live. `tile_cols`: of the tiles of one device-block, at most 2 have column blocks among one device-block's 6 columns (c // 6 equal); every device-block reaches 2 for some such column device-block, and every column device-block receives 2 from some device-block.
All inputs are finite; a program needn't handle non-finite values. No bound on the sum of `row_kind` on one device may be relied on, other than what follows from the above.
Results may differ from the reference program's by a relative error of at most 0.00073.
Values may be sent and summed in bfloat16 or wider, within the bound.
A program may use at most 64 MiB of HBM per device.

```python
import math
import jax
import jax.numpy as jnp
from jax import lax

BLOCK = 256
TILES_DEV = 32
RB_DEV = 4
CB_DEV = 6
ITERS = 2
TILES = 512
ROW_BLOCKS = 64
COL_BLOCKS = 96
N_ROWS = 16


def rising_field(key, blocks):
    ramp = 2.0 ** (2.0 * jnp.arange(blocks, dtype=jnp.float32) / max(blocks - 1, 1))
    values = jnp.clip(jax.random.normal(key, (blocks, BLOCK), jnp.float32), -4.0, 4.0)
    return values * ramp[:, None]


def draw_right_side(key, part):
    key = jax.random.fold_in(key, 11)
    return rising_field(key, ROW_BLOCKS)


def draw_cost(key, part):
    key = jax.random.fold_in(key, 12)
    return rising_field(key, COL_BLOCKS)


def draw_tile_count(key, part):
    key = jax.random.fold_in(key, 13)
    first, second = jax.random.split(key)
    counts = jax.random.randint(first, (N_ROWS,), TILES_DEV // 2, TILES_DEV + 1)
    where_full = jax.random.randint(second, (), 0, N_ROWS)
    return counts.at[where_full].set(TILES_DEV).astype(jnp.int32)


def draw_tile_cols(key, part):
    key = jax.random.fold_in(key, 14)
    first, second = jax.random.split(key)
    device_keys = jax.random.split(first, N_ROWS)
    orders = jax.vmap(lambda one: jax.random.permutation(one, N_ROWS))(device_keys)
    picks = jnp.arange(TILES_DEV, dtype=jnp.int32) % N_ROWS
    owners = orders[:, picks]
    within = jax.random.randint(second, (N_ROWS, TILES_DEV), 0, CB_DEV)
    return (owners * CB_DEV + within).reshape(N_ROWS * TILES_DEV).astype(jnp.int32)


def place_ends(drawn, own_key, low, top_value):
    longest = drawn.shape.index(max(drawn.shape))
    spots = []
    for shift in (0, 1):
        where = [jax.random.randint(jax.random.fold_in(own_key, axis), (), 0, length) for axis, length in enumerate(drawn.shape)]
        where[longest] = (where[longest] + shift) % drawn.shape[longest]
        spots.append(tuple(where))
    return drawn.at[spots[0]].set(low).at[spots[1]].set(top_value)


def steps_of(rng, dims, cuts, smallest, high):
    loudness = 1.0
    for position, shards_of in cuts:
        draws = jax.random.uniform(jax.random.fold_in(jax.random.fold_in(rng, 6), position), (shards_of,), jnp.float32, smallest / len(cuts), high / len(cuts))
        loudness = loudness * jnp.repeat(jnp.exp(draws), dims[position] // shards_of).reshape((-1,) + (1,) * (len(dims) - 1 - position))
    return loudness


def normal_values(stream_key, shape, deviation, most, cuts=(), kind=jnp.bfloat16):
    factor_of = steps_of(stream_key, shape, cuts, -0.22, 0.18) if cuts else 1.0
    result = jax.random.normal(stream_key, shape, jnp.float32) * deviation * factor_of
    return jnp.minimum(jnp.maximum(result, -most), most).astype(kind)


def setup_inputs(seed: int = 0, part: int = 0) -> dict:
    keys = jax.random.split(jax.random.key(seed), 11)
    own_keys = jax.random.split(jax.random.fold_in(keys[10], part), 11)
    return {
        "tiles": normal_values(own_keys[0], (TILES, BLOCK, BLOCK), BLOCK ** -0.5, 0.375, ((0, 16),)),
        "tile_rows": place_ends(jax.random.randint(own_keys[1], (TILES,), 0, RB_DEV), jax.random.fold_in(own_keys[1], 1), 0, RB_DEV - 1).astype(jnp.int32),
        "tile_cols": draw_tile_cols(jax.random.fold_in(jax.random.fold_in(keys[10], part), 71), part),
        "tile_count": draw_tile_count(jax.random.fold_in(jax.random.fold_in(keys[10], part), 71), part),
        "right_side": draw_right_side(jax.random.fold_in(jax.random.fold_in(keys[10], part), 71), part),
        "row_kind": place_ends((jax.random.randint(own_keys[5], (ROW_BLOCKS, BLOCK), 0, 2) < 1).astype(jnp.int32), jax.random.fold_in(own_keys[5], 1), 0, 1),
        "cost": draw_cost(jax.random.fold_in(jax.random.fold_in(keys[10], part), 71), part),
        "upper": jnp.clip(jnp.exp(math.log(2.0) - 3.6888794 * jax.random.uniform(own_keys[7], (COL_BLOCKS, BLOCK), jnp.float32) ** steps_of(own_keys[7], (COL_BLOCKS, BLOCK), ((0, 16),), -0.2, 0.2)), 0.05, 2.0),
        "primal_init": jnp.clip(1.0 * jax.random.uniform(own_keys[8], (COL_BLOCKS, BLOCK), jnp.float32) ** steps_of(own_keys[8], (COL_BLOCKS, BLOCK), ((0, 16),), -0.2, 0.2), 0.0, 1.0),
        "dual_init": normal_values(own_keys[9], (ROW_BLOCKS, BLOCK), 0.5, 3.0, ((0, 16),), jnp.float32),
    }


primal_step = 0.1
dual_step = 0.1

def live_mask(tile_count):
    slots = jnp.arange(N_ROWS * TILES_DEV, dtype=jnp.int32)
    return (slots % TILES_DEV < tile_count[slots // TILES_DEV]).astype(jnp.float32)

def row_owner(tile_rows):
    slots = jnp.arange(N_ROWS * TILES_DEV, dtype=jnp.int32)
    return (slots // TILES_DEV * RB_DEV + tile_rows).astype(jnp.int32)

def forward(tiles, vector, owner, tile_cols, live):
    picked = vector[tile_cols].astype(jnp.float32).reshape(N_ROWS, TILES_DEV, BLOCK)
    stacked = tiles.reshape(N_ROWS, TILES_DEV, BLOCK, BLOCK)
    parts = lax.map(lambda pair: jnp.einsum('tij,tj->ti', pair[0].astype(jnp.float32), pair[1], precision=lax.Precision.HIGHEST), (stacked, picked))
    parts = parts.reshape(N_ROWS * TILES_DEV, BLOCK) * live[:, None]
    return jax.ops.segment_sum(parts, owner, num_segments=ROW_BLOCKS)

def adjoint(tiles, vector, owner, tile_cols, live):
    picked = vector[owner].astype(jnp.float32).reshape(N_ROWS, TILES_DEV, BLOCK)
    stacked = tiles.reshape(N_ROWS, TILES_DEV, BLOCK, BLOCK)
    parts = lax.map(lambda pair: jnp.einsum('tij,ti->tj', pair[0].astype(jnp.float32), pair[1], precision=lax.Precision.HIGHEST), (stacked, picked))
    parts = parts.reshape(N_ROWS * TILES_DEV, BLOCK) * live[:, None]
    return jax.ops.segment_sum(parts, tile_cols, num_segments=COL_BLOCKS)

def reference(tiles, tile_rows, tile_cols, tile_count, right_side, row_kind, cost, upper, primal_init, dual_init):
    live = live_mask(tile_count)
    owner = row_owner(tile_rows)
    primal_x = primal_init
    dual_y = dual_init
    row_image = forward(tiles, primal_x.astype(jnp.bfloat16), owner, tile_cols, live)
    col_image = adjoint(tiles, dual_y.astype(jnp.bfloat16), owner, tile_cols, live)
    bounded = row_kind == 1
    results = []
    for step in range(ITERS):
        x_new = jnp.clip(primal_x - primal_step * (cost - col_image), 0.0, upper)
        x_bar = (2.0 * x_new - primal_x).astype(jnp.bfloat16)
        bar_image = forward(tiles, x_bar, owner, tile_cols, live)
        row_image = (bar_image + row_image) / 2.0
        y_new = dual_y + dual_step * (right_side - bar_image)
        y_new = jnp.where(bounded, jnp.maximum(y_new, 0.0), y_new)
        violation = right_side - row_image
        violation = jnp.where(bounded, jnp.maximum(violation, 0.0), violation)
        primal_sum = jnp.sum(violation * violation)
        col_image = adjoint(tiles, y_new.astype(jnp.bfloat16), owner, tile_cols, live)
        gap = x_new - jnp.clip(x_new - (cost - col_image), 0.0, upper)
        dual_sum = jnp.sum(gap * gap)
        results.append(jnp.stack([jnp.sqrt(primal_sum / (ROW_BLOCKS * BLOCK)), jnp.sqrt(dual_sum / (COL_BLOCKS * BLOCK))]))
        primal_x = x_new
        dual_y = y_new
    return (primal_x, dual_y, jnp.stack(results))
```

```python
import functools

import jax
import jax.numpy as jnp
from jax import lax
from jax.experimental import pallas as pl
from jax.experimental.pallas import tpu as pltpu
from jax.sharding import PartitionSpec as P

ITERS = 2
PRIMAL_STEP = 0.1
DUAL_STEP = 0.1
LANES = 128
MSG = 8
CHUNKS = 4
MESH = pl.DeviceIdType.MESH


def kernel(
    devices,
    rows_s,
    cols_s,
    count_s,
    tiles_h,
    right_h,
    kind_h,
    cost_h,
    upper_h,
    x_h,
    y_h,
    x_out,
    y_out,
    norm_out,
    tiles_v,
    right_v,
    kind_v,
    cost_v,
    upper_v,
    x_v,
    y_v,
    yb_v,
    peer_v,
    base_v,
    target_v,
    pick_v,
    send,
    recv,
    small_sem,
    tile_sem,
    send_sem,
    recv_sem,
):
    slots, block = tiles_v.shape[0], tiles_v.shape[1]
    row_count, col_count = right_v.shape[0], cost_v.shape[0]
    halves = block // LANES
    capacity = -(-slots // devices)
    per_vector = halves * capacity
    places = devices * capacity
    span = MSG * devices
    per_chunk = slots // CHUNKS
    me = lax.axis_index("rows")

    def peer_of(step):
        return lax.rem(me + step, devices)

    def each_peer(do):
        if devices <= 16:
            for step in range(1, devices):
                do(step)
        else:
            pl.loop(1, devices)(do)

    chunk_copies = []
    for c in range(CHUNKS):
        part = pl.ds(c * per_chunk, per_chunk)
        chunk_copies.append(
            pltpu.make_async_copy(tiles_h.at[part], tiles_v.at[part], tile_sem.at[c])
        )
    small_copies = []
    pairs = (
        (y_h, y_v),
        (cost_h, cost_v),
        (upper_h, upper_v),
        (x_h, x_v),
        (right_h, right_v),
        (kind_h, kind_v),
    )
    for n, (src, dst) in enumerate(pairs):
        small_copies.append(pltpu.make_async_copy(src, dst, small_sem.at[n]))
    small_copies[0].start()
    for copy in chunk_copies:
        copy.start()
    for copy in small_copies[1:]:
        copy.start()

    barrier = pltpu.get_barrier_semaphore()

    def greet(step):
        pl.semaphore_signal(
            barrier, inc=1, device_id={"rows": peer_of(step)}, device_id_type=MESH
        )

    each_peer(greet)

    lane = lax.broadcasted_iota(jnp.int32, (slots, LANES), 1)
    sub = lax.broadcasted_iota(jnp.int32, (slots, LANES), 0)
    lane1 = lax.broadcasted_iota(jnp.int32, (1, LANES), 1)
    peer_l = jnp.full((1, LANES), -1, jnp.int32)
    local_l = jnp.zeros((1, LANES), jnp.int32)
    for t in range(slots):
        col = cols_s[t]
        owner = col // col_count
        local = col - owner * col_count
        step = owner - me
        step = jnp.where(step < 0, step + devices, step)
        step = jnp.where(t < count_s[0], step, 16 * devices + t)
        peer_v[t : t + 1, :] = jnp.full((1, LANES), step, jnp.int32)
        peer_l = jnp.where(lane1 == t, step, peer_l)
        local_l = jnp.where(lane1 == t, local, local_l)
    peer_s = peer_v[...]
    same = peer_s == peer_l
    rank_s = jnp.sum(jnp.where(same & (lane < sub), 1.0, 0.0), axis=1, keepdims=True)
    rank_l = jnp.sum(jnp.where(same & (sub < lane), 1.0, 0.0), axis=0, keepdims=True)
    rank_s = rank_s.astype(jnp.int32)
    base_v[...] = peer_s * MSG + rank_s
    target_v[...] = peer_s + rank_s * devices
    target_l = peer_l + rank_l.astype(jnp.int32) * devices

    place = lax.broadcasted_iota(jnp.int32, (places, LANES), 0)
    found = (target_l == place) & (
        lax.broadcasted_iota(jnp.int32, (places, LANES), 1) < slots
    )
    col_of = jnp.sum(
        jnp.where(found, (local_l + 1).astype(jnp.float32), 0.0), axis=1, keepdims=True
    )
    col_of = jnp.broadcast_to(col_of - 1.0, (places, LANES))
    send[...] = jnp.zeros_like(send)
    for s in range(capacity):
        send[0, pl.ds(per_vector + s, devices, stride=MSG), :] = col_of[
            s * devices : (s + 1) * devices
        ]

    wide_lane = lax.broadcasted_iota(jnp.int32, (16, span), 1)
    wide_sub = lax.broadcasted_iota(jnp.int32, (16, span), 0)
    vector_of = wide_sub // row_count
    row_of = jnp.where(vector_of < 2, wide_sub - vector_of * row_count, -1)
    wanted = wide_lane - vector_of * per_vector
    for t in range(slots):
        base = base_v[t : t + 1, :]
        if span > LANES:
            base = jnp.concatenate([base] * (span // LANES), axis=1)
        hit_row = row_of == rows_s[t]
        for h in range(halves):
            hit = hit_row & (wanted == base + h * capacity)
            pick_v[h, t * 16 : (t + 1) * 16, :] = jnp.where(hit, 1.0, 0.0).astype(
                jnp.bfloat16
            )

    place_wide = lax.broadcasted_iota(jnp.int32, (places, block), 0)

    def adjoint(first):
        total = jnp.zeros((places, block), jnp.float32)
        for c in range(CHUNKS):
            if first:
                chunk_copies[c].wait()
            parts = []
            for t in range(c * per_chunk, (c + 1) * per_chunk):
                row = yb_v[pl.ds(rows_s[t], 1), :]
                target = target_v[t : t + 1, :]
                target = jnp.concatenate([target] * halves, axis=1)
                parts.append(
                    jnp.where(target == place_wide, row, 0.0).astype(jnp.bfloat16)
                )
            left = jnp.concatenate(parts, axis=1)
            right = tiles_v[c * per_chunk : (c + 1) * per_chunk].reshape(
                per_chunk * block, block
            )
            total += jnp.dot(left, right, preferred_element_type=jnp.float32)
        return total

    def forward(e):
        arrived = recv[e].astype(jnp.bfloat16)
        picked = [
            jnp.dot(pick_v[h], arrived, preferred_element_type=jnp.float32).astype(
                jnp.bfloat16
            )
            for h in range(halves)
        ]
        total = jnp.zeros((16, block), jnp.float32)
        for t in range(slots):
            left = jnp.concatenate([p[t * 16 : (t + 1) * 16] for p in picked], axis=1)
            total += lax.dot_general(
                left, tiles_v[t], (((1,), (1,)), ((), ())), preferred_element_type=jnp.float32
            )
        return total

    def exchange(e):
        recv[e, 0:MSG, :] = send[e, 0:MSG, :]

        def go(step):
            pltpu.make_async_remote_copy(
                src_ref=send.at[e, pl.ds(pl.multiple_of(MSG * step, MSG), MSG)],
                dst_ref=recv.at[e, pl.ds(pl.multiple_of(MSG * (devices - step), MSG), MSG)],
                send_sem=send_sem.at[e],
                recv_sem=recv_sem.at[e],
                device_id={"rows": peer_of(step)},
                device_id_type=MESH,
            ).start()

        each_peer(go)

    def settle(buffer, sems, e):
        rest = buffer.at[e, pl.ds(MSG, span - MSG)]
        pltpu.make_async_copy(rest, rest, sems.at[e]).wait()

    def send_terms(e, terms):
        for s in range(capacity):
            for h in range(halves):
                send[e, pl.ds(h * capacity + s, devices, stride=MSG), :] = terms[
                    s * devices : (s + 1) * devices, h * LANES : (h + 1) * LANES
                ]
        exchange(e)

    sub8 = lax.broadcasted_iota(jnp.int32, (MSG, LANES), 0).astype(jnp.float32)

    def column_image(e):
        sums = [[jnp.zeros((MSG, LANES), jnp.float32) for _ in range(2)] for _ in range(halves)]
        count = 0
        for k in range(devices):
            for s in range(capacity):
                at = k * MSG + per_vector + s
                hit = recv[0, at : at + 1, :] == sub8
                for h in range(halves):
                    at = k * MSG + h * capacity + s
                    term = jnp.where(hit, recv[e, at : at + 1, :], 0.0)
                    sums[h][count % 2] += term
                count += 1
        whole = jnp.concatenate([a + b for a, b in sums], axis=1)
        return whole[:col_count]

    def put_vector(e, v, x):
        for s in range(capacity):
            asked = recv[0, pl.ds(per_vector + s, devices, stride=MSG), :]
            for h in range(halves):
                reply = jnp.zeros((devices, LANES), jnp.float32)
                for c in range(col_count):
                    reply = jnp.where(
                        asked == float(c), x[c : c + 1, h * LANES : (h + 1) * LANES], reply
                    )
                at = v * per_vector + h * capacity + s
                send[e, pl.ds(at, devices, stride=MSG), :] = reply

    def rounded(x):
        return x.astype(jnp.bfloat16).astype(jnp.float32)

    def lane_sum(x):
        x = jnp.sum(x * x, axis=0, keepdims=True)
        total = x[:, :LANES]
        for h in range(1, halves):
            total += x[:, h * LANES : (h + 1) * LANES]
        return total

    small_copies[0].wait()
    y = y_v[...]
    yb_v[...] = rounded(y)
    terms = adjoint(True)
    pl.semaphore_wait(barrier, devices - 1)
    send_terms(0, terms)
    for copy in small_copies[1:]:
        copy.wait()
    cost, upper, x = cost_v[...], upper_v[...], x_v[...]
    right = right_v[...]
    bounded = kind_v[...] == 1
    settle(recv, recv_sem, 0)
    put_vector(1, 1, rounded(x))
    col_image = column_image(0)
    last = 2 * ITERS + 1
    row_image = None
    for step in range(ITERS):
        out, back = 2 * step + 1, 2 * step + 2
        x_new = jnp.clip(x - PRIMAL_STEP * (cost - col_image), 0.0, upper)
        put_vector(out, 0, rounded(2.0 * x_new - x))
        exchange(out)
        settle(recv, recv_sem, out)
        images = forward(out)
        bar_image = images[:row_count]
        if step == 0:
            row_image = images[row_count : 2 * row_count]
        row_image = (bar_image + row_image) / 2.0
        y_new = y + DUAL_STEP * (right - bar_image)
        y_new = jnp.where(bounded, jnp.maximum(y_new, 0.0), y_new)
        yb_v[...] = rounded(y_new)
        send_terms(back, adjoint(False))
        violation = right - row_image
        violation = jnp.where(bounded, jnp.maximum(violation, 0.0), violation)
        send[last, 2 * step : 2 * step + 1, :] = lane_sum(violation)
        settle(recv, recv_sem, back)
        col_image = column_image(back)
        gap = x_new - jnp.clip(x_new - (cost - col_image), 0.0, upper)
        send[last, 2 * step + 1 : 2 * step + 2, :] = lane_sum(gap)
        x, y = x_new, y_new

    recv[last, 0:MSG, :] = send[last, 0:MSG, :]

    def tell(step):
        pltpu.make_async_remote_copy(
            src_ref=send.at[last, pl.ds(0, MSG)],
            dst_ref=recv.at[last, pl.ds(pl.multiple_of(MSG * (devices - step), MSG), MSG)],
            send_sem=send_sem.at[last],
            recv_sem=recv_sem.at[last],
            device_id={"rows": peer_of(step)},
            device_id_type=MESH,
        ).start()

    each_peer(tell)
    x_out[...] = x
    y_out[...] = y
    for e in range(last):
        settle(send, send_sem, e)
    settle(recv, recv_sem, last)
    sums = jnp.sum(recv[last].reshape(devices, MSG, LANES), axis=0)
    sums = jnp.sum(sums, axis=1, keepdims=True)
    kinds = lax.broadcasted_iota(jnp.int32, (MSG, 1), 0)
    row_scale = 1.0 / (row_count * devices * block)
    col_scale = 1.0 / (col_count * devices * block)
    scale = jnp.where(kinds % 2 == 0, row_scale, col_scale)
    roots = jnp.sqrt(sums * scale)
    side = lax.broadcasted_iota(jnp.int32, (1, 2), 1)
    for step in range(ITERS):
        norm_out[step : step + 1, :] = jnp.where(
            side == 0, roots[2 * step : 2 * step + 1], roots[2 * step + 1 : 2 * step + 2]
        )
    settle(send, send_sem, last)


def per_device(
    tiles,
    tile_rows,
    tile_cols,
    tile_count,
    right_side,
    row_kind,
    cost,
    upper,
    primal_init,
    dual_init,
):
    devices = lax.axis_size("rows")
    slots, block = tiles.shape[0], tiles.shape[1]
    span = MSG * devices
    exchanges = 2 * ITERS + 2
    f32, i32 = jnp.float32, jnp.int32
    smem = pl.BlockSpec(memory_space=pltpu.SMEM)
    anywhere = pl.BlockSpec(memory_space=pl.ANY)
    vmem = pl.BlockSpec(memory_space=pltpu.VMEM)
    places = devices * (-(-slots // devices))
    call = pl.pallas_call(
        functools.partial(kernel, devices),
        out_shape=(
            jax.ShapeDtypeStruct(primal_init.shape, f32),
            jax.ShapeDtypeStruct(dual_init.shape, f32),
            jax.ShapeDtypeStruct((ITERS, 2), f32),
        ),
        in_specs=[smem] * 3 + [anywhere] * 7,
        out_specs=(vmem, vmem, vmem),
        scratch_shapes=[
            pltpu.VMEM(tiles.shape, tiles.dtype),
            pltpu.VMEM(right_side.shape, f32),
            pltpu.VMEM(row_kind.shape, i32),
            pltpu.VMEM(cost.shape, f32),
            pltpu.VMEM(upper.shape, f32),
            pltpu.VMEM(primal_init.shape, f32),
            pltpu.VMEM(dual_init.shape, f32),
            pltpu.VMEM(dual_init.shape, f32),
            pltpu.VMEM((slots, LANES), i32),
            pltpu.VMEM((slots, LANES), i32),
            pltpu.VMEM((slots, LANES), i32),
            pltpu.VMEM((block // LANES, slots * 16, span), jnp.bfloat16),
            pltpu.VMEM((exchanges, span, LANES), f32),
            pltpu.VMEM((exchanges, span, LANES), f32),
            pltpu.SemaphoreType.DMA((6,)),
            pltpu.SemaphoreType.DMA((CHUNKS,)),
            pltpu.SemaphoreType.DMA((exchanges,)),
            pltpu.SemaphoreType.DMA((exchanges,)),
        ],
        compiler_params=pltpu.CompilerParams(
            collective_id=0, has_side_effects=True, vmem_limit_bytes=40 * 1024 * 1024
        ),
        name="pdhg",
    )
    return call(
        tile_rows,
        tile_cols,
        tile_count,
        tiles,
        right_side,
        row_kind,
        cost,
        upper,
        primal_init,
        dual_init,
    )


def solution(mesh):
    return jax.shard_map(
        per_device,
        mesh=mesh,
        in_specs=(
            P(("groups", "rows"), None, None),
            P(("groups", "rows")),
            P(("groups", "rows")),
            P(("groups", "rows")),
            P(("groups", "rows"), None),
            P(("groups", "rows"), None),
            P(("groups", "rows"), None),
            P(("groups", "rows"), None),
            P(("groups", "rows"), None),
            P(("groups", "rows"), None),
        ),
        out_specs=(P(("groups", "rows"), None), P(("groups", "rows"), None), P("groups", None)),
        check_vma=False,
    )
```

```python
import functools

import jax
import jax.numpy as jnp
from jax import lax
from jax.experimental import pallas as pl
from jax.experimental.pallas import tpu as pltpu
from jax.sharding import PartitionSpec as P

ITERS = 2
PRIMAL_STEP = 0.1
DUAL_STEP = 0.1
LANES = 128
MSG = 8
CHUNKS = 4
MESH = pl.DeviceIdType.MESH


def kernel(
    devices,
    rows_h,
    cols_h,
    count_h,
    tiles_h,
    right_h,
    kind_h,
    cost_h,
    upper_h,
    x_h,
    y_h,
    x_out,
    y_out,
    norm_out,
    rows_s,
    cols_s,
    count_s,
    tiles_v,
    flipped_v,
    right_v,
    kind_v,
    cost_v,
    upper_v,
    x_v,
    y_v,
    yb_v,
    peer_v,
    base_v,
    target_v,
    pick_v,
    send,
    recv,
    small_sem,
    tile_sem,
    send_sem,
    recv_sem,
):
    slots, block = tiles_v.shape[0], tiles_v.shape[1]
    row_count, col_count = right_v.shape[0], cost_v.shape[0]
    halves = block // LANES
    capacity = -(-slots // devices)
    per_vector = halves * capacity
    places = devices * capacity
    span = MSG * devices
    per_chunk = slots // CHUNKS
    me = lax.axis_index("rows")

    bits = devices.bit_length() - 1
    if devices != 1 << bits or per_vector * 2 > MSG or col_count > MSG:
        raise ValueError("unsupported sizes")

    def peer_of(step):
        peer = me
        for b in range(bits):
            one = 1 << b
            peer += ((step // one) % 2) * one * (1 - 2 * ((me // one) % 2))
        return peer

    def each_peer(do):
        if devices <= 16:
            for step in reversed(range(1, devices)):
                do(step)
        else:
            pl.loop(0, devices - 1)(lambda i: do(devices - 1 - i))

    barrier = pltpu.get_barrier_semaphore()

    def greet(step):
        pl.semaphore_signal(
            barrier, inc=1, device_id={"rows": peer_of(step)}, device_id_type=MESH
        )

    each_peer(greet)

    chunk_copies = []
    for c in range(CHUNKS):
        part = pl.ds(c * per_chunk, per_chunk)
        chunk_copies.append(
            pltpu.make_async_copy(tiles_h.at[part], tiles_v.at[part], tile_sem.at[c])
        )
    small_copies = []
    pairs = (
        (cols_h, cols_s),
        (count_h, count_s),
        (rows_h, rows_s),
        (y_h, y_v),
        (cost_h, cost_v),
        (upper_h, upper_v),
        (x_h, x_v),
        (right_h, right_v),
        (kind_h, kind_v),
    )
    for n, (src, dst) in enumerate(pairs):
        small_copies.append(pltpu.make_async_copy(src, dst, small_sem.at[n]))
    for copy in small_copies[:4]:
        copy.start()
    for copy in chunk_copies:
        copy.start()
    for copy in small_copies[4:]:
        copy.start()

    for copy in small_copies[:3]:
        copy.wait()

    lane = lax.broadcasted_iota(jnp.int32, (slots, LANES), 1)
    sub = lax.broadcasted_iota(jnp.int32, (slots, LANES), 0)
    lane1 = lax.broadcasted_iota(jnp.int32, (1, LANES), 1)
    peer_l = jnp.full((1, LANES), -1, jnp.int32)
    local_l = jnp.zeros((1, LANES), jnp.int32)
    for t in range(slots):
        col = cols_s[t]
        owner = col // col_count
        local = col - owner * col_count
        step = 0
        for b in range(bits):
            one = 1 << b
            step += ((owner // one + me // one) % 2) * one
        step = jnp.where(t < count_s[0], step, 16 * devices + t)
        peer_v[t : t + 1, :] = jnp.full((1, LANES), step, jnp.int32)
        peer_l = jnp.where(lane1 == t, step, peer_l)
        local_l = jnp.where(lane1 == t, local, local_l)
    peer_s = peer_v[...]
    same = peer_s == peer_l
    rank_s = jnp.sum(jnp.where(same & (lane < sub), 1.0, 0.0), axis=1, keepdims=True)
    rank_l = jnp.sum(jnp.where(same & (sub < lane), 1.0, 0.0), axis=0, keepdims=True)
    rank_s = rank_s.astype(jnp.int32)
    base_v[...] = peer_s * MSG + rank_s
    target_v[...] = peer_s + rank_s * devices
    target_l = peer_l + rank_l.astype(jnp.int32) * devices

    place = lax.broadcasted_iota(jnp.int32, (places, LANES), 0)
    found = (target_l == place) & (
        lax.broadcasted_iota(jnp.int32, (places, LANES), 1) < slots
    )
    col_of = jnp.sum(
        jnp.where(found, (local_l + 1).astype(jnp.float32), 0.0), axis=1, keepdims=True
    )
    col_of = jnp.broadcast_to(col_of - 1.0, (places, LANES))
    for s in range(capacity):
        send[0, pl.ds(per_vector + s, devices, stride=MSG), :] = col_of[
            s * devices : (s + 1) * devices
        ]

    wide_lane = lax.broadcasted_iota(jnp.int32, (16, span), 1)
    wide_sub = lax.broadcasted_iota(jnp.int32, (16, span), 0)
    vector_of = wide_sub // row_count
    row_of = jnp.where(vector_of < 2, wide_sub - vector_of * row_count, -1)
    wanted = wide_lane - vector_of * per_vector
    for t in range(slots):
        base = base_v[t : t + 1, :]
        if span > LANES:
            base = jnp.concatenate([base] * (span // LANES), axis=1)
        hit_row = row_of == rows_s[t]
        for h in range(halves):
            hit = hit_row & (wanted == base + h * capacity)
            pick_v[h, t * 16 : (t + 1) * 16, :] = jnp.where(hit, 1.0, 0.0).astype(
                jnp.bfloat16
            )

    place_wide = lax.broadcasted_iota(jnp.int32, (places, block), 0)

    def adjoint(first):
        total = jnp.zeros((places, block), jnp.float32)
        for c in range(CHUNKS):
            if first:
                chunk_copies[c].wait()
            parts = []
            for t in range(c * per_chunk, (c + 1) * per_chunk):
                row = yb_v[pl.ds(rows_s[t], 1), :]
                target = target_v[t : t + 1, :]
                target = jnp.concatenate([target] * halves, axis=1)
                parts.append(
                    jnp.where(target == place_wide, row, 0.0).astype(jnp.bfloat16)
                )
            left = jnp.concatenate(parts, axis=1)
            right = tiles_v[c * per_chunk : (c + 1) * per_chunk].reshape(
                per_chunk * block, block
            )
            total += jnp.dot(left, right, preferred_element_type=jnp.float32)
        return total

    message_row = lax.broadcasted_iota(jnp.int32, (span, LANES), 0) % MSG

    def forward(e):
        arrived = jnp.where(message_row < used[e], recv[e], 0.0).astype(jnp.bfloat16)
        picked = [
            jnp.dot(pick_v[h], arrived, preferred_element_type=jnp.float32).astype(
                jnp.bfloat16
            )
            for h in range(halves)
        ]
        total = jnp.zeros((16, block), jnp.float32)
        for c in range(CHUNKS):
            parts = []
            for t in range(c * per_chunk, (c + 1) * per_chunk):
                parts += [p[t * 16 : (t + 1) * 16] for p in picked]
            left = jnp.concatenate(parts, axis=1)
            right = flipped_v[c * per_chunk : (c + 1) * per_chunk].reshape(
                per_chunk * block, block
            )
            total += jnp.dot(left, right, preferred_element_type=jnp.float32)
        return total

    used = [per_vector] * (2 * ITERS + 2)
    used[0], used[1], used[-1] = per_vector + capacity, 2 * per_vector, 2 * ITERS

    def exchange(e):
        recv[e, 0 : used[e], :] = send[e, 0 : used[e], :]

        def go(step):
            pltpu.make_async_remote_copy(
                src_ref=send.at[e, pl.ds(pl.multiple_of(MSG * step, MSG), used[e])],
                dst_ref=recv.at[e, pl.ds(pl.multiple_of(MSG * step, MSG), used[e])],
                send_sem=send_sem.at[e],
                recv_sem=recv_sem.at[e],
                device_id={"rows": peer_of(step)},
                device_id_type=MESH,
            ).start()

        each_peer(go)

    def settle(buffer, sems, e):
        rest = buffer.at[e, pl.ds(MSG, (devices - 1) * used[e])]
        pltpu.make_async_copy(rest, rest, sems.at[e]).wait()

    def send_terms(e, terms):
        for s in range(capacity):
            for h in range(halves):
                send[e, pl.ds(h * capacity + s, devices, stride=MSG), :] = terms[
                    s * devices : (s + 1) * devices, h * LANES : (h + 1) * LANES
                ]
        exchange(e)

    sub8 = lax.broadcasted_iota(jnp.int32, (MSG, LANES), 0).astype(jnp.float32)

    def column_image(e):
        sums = [[jnp.zeros((MSG, LANES), jnp.float32) for _ in range(2)] for _ in range(halves)]
        count = 0
        for k in range(devices):
            for s in range(capacity):
                at = k * MSG + per_vector + s
                hit = recv[0, at : at + 1, :] == sub8
                for h in range(halves):
                    at = k * MSG + h * capacity + s
                    term = jnp.where(hit, recv[e, at : at + 1, :], 0.0)
                    sums[h][count % 2] += term
                count += 1
        whole = jnp.concatenate([a + b for a, b in sums], axis=1)
        return whole[:col_count]

    def put_vector(e, v, x):
        for s in range(capacity):
            asked = recv[0, pl.ds(per_vector + s, devices, stride=MSG), :]
            for h in range(halves):
                reply = jnp.zeros((devices, LANES), jnp.float32)
                for c in range(col_count):
                    reply = jnp.where(
                        asked == float(c), x[c : c + 1, h * LANES : (h + 1) * LANES], reply
                    )
                at = v * per_vector + h * capacity + s
                send[e, pl.ds(at, devices, stride=MSG), :] = reply

    def rounded(x):
        return x.astype(jnp.bfloat16).astype(jnp.float32)

    def lane_sum(x):
        x = jnp.sum(x * x, axis=0, keepdims=True)
        total = x[:, :LANES]
        for h in range(1, halves):
            total += x[:, h * LANES : (h + 1) * LANES]
        return total

    small_copies[3].wait()
    y = y_v[...]
    yb_v[...] = rounded(y)
    terms = adjoint(True)
    pl.semaphore_wait(barrier, devices - 1)
    send_terms(0, terms)
    for t in range(slots):
        flipped_v[t] = tiles_v[t].T
    for copy in small_copies[4:]:
        copy.wait()
    cost, upper, x = cost_v[...], upper_v[...], x_v[...]
    right = right_v[...]
    bounded = kind_v[...] == 1
    settle(recv, recv_sem, 0)
    put_vector(1, 1, rounded(x))
    col_image = column_image(0)
    last = 2 * ITERS + 1
    row_image = None
    for step in range(ITERS):
        out, back = 2 * step + 1, 2 * step + 2
        x_new = jnp.clip(x - PRIMAL_STEP * (cost - col_image), 0.0, upper)
        put_vector(out, 0, rounded(2.0 * x_new - x))
        exchange(out)
        settle(recv, recv_sem, out)
        images = forward(out)
        bar_image = images[:row_count]
        if step == 0:
            row_image = images[row_count : 2 * row_count]
        row_image = (bar_image + row_image) / 2.0
        y_new = y + DUAL_STEP * (right - bar_image)
        y_new = jnp.where(bounded, jnp.maximum(y_new, 0.0), y_new)
        yb_v[...] = rounded(y_new)
        send_terms(back, adjoint(False))
        violation = right - row_image
        violation = jnp.where(bounded, jnp.maximum(violation, 0.0), violation)
        send[last, 2 * step : 2 * step + 1, :] = lane_sum(violation)
        settle(recv, recv_sem, back)
        col_image = column_image(back)
        gap = x_new - jnp.clip(x_new - (cost - col_image), 0.0, upper)
        send[last, 2 * step + 1 : 2 * step + 2, :] = lane_sum(gap)
        x, y = x_new, y_new

    recv[last, 0 : used[last], :] = send[last, 0 : used[last], :]

    def tell(step):
        pltpu.make_async_remote_copy(
            src_ref=send.at[last, pl.ds(0, used[last])],
            dst_ref=recv.at[last, pl.ds(pl.multiple_of(MSG * step, MSG), used[last])],
            send_sem=send_sem.at[last],
            recv_sem=recv_sem.at[last],
            device_id={"rows": peer_of(step)},
            device_id_type=MESH,
        ).start()

    each_peer(tell)
    x_out[...] = x
    y_out[...] = y
    for e in range(last):
        settle(send, send_sem, e)
    settle(recv, recv_sem, last)
    sums = jnp.sum(recv[last].reshape(devices, MSG, LANES), axis=0)
    sums = jnp.sum(sums, axis=1, keepdims=True)
    kinds = lax.broadcasted_iota(jnp.int32, (MSG, 1), 0)
    row_scale = 1.0 / (row_count * devices * block)
    col_scale = 1.0 / (col_count * devices * block)
    scale = jnp.where(kinds % 2 == 0, row_scale, col_scale)
    roots = jnp.sqrt(sums * scale)
    side = lax.broadcasted_iota(jnp.int32, (1, 2), 1)
    for step in range(ITERS):
        norm_out[step : step + 1, :] = jnp.where(
            side == 0, roots[2 * step : 2 * step + 1], roots[2 * step + 1 : 2 * step + 2]
        )
    settle(send, send_sem, last)


def per_device(
    tiles,
    tile_rows,
    tile_cols,
    tile_count,
    right_side,
    row_kind,
    cost,
    upper,
    primal_init,
    dual_init,
):
    devices = lax.axis_size("rows")
    slots, block = tiles.shape[0], tiles.shape[1]
    span = MSG * devices
    exchanges = 2 * ITERS + 2
    f32, i32 = jnp.float32, jnp.int32
    anywhere = pl.BlockSpec(memory_space=pl.ANY)
    vmem = pl.BlockSpec(memory_space=pltpu.VMEM)
    places = devices * (-(-slots // devices))
    call = pl.pallas_call(
        functools.partial(kernel, devices),
        out_shape=(
            jax.ShapeDtypeStruct(primal_init.shape, f32),
            jax.ShapeDtypeStruct(dual_init.shape, f32),
            jax.ShapeDtypeStruct((ITERS, 2), f32),
        ),
        in_specs=[anywhere] * 10,
        out_specs=(vmem, vmem, vmem),
        scratch_shapes=[
            pltpu.SMEM(tile_rows.shape, i32),
            pltpu.SMEM(tile_cols.shape, i32),
            pltpu.SMEM(tile_count.shape, i32),
            pltpu.VMEM(tiles.shape, tiles.dtype),
            pltpu.VMEM(tiles.shape, tiles.dtype),
            pltpu.VMEM(right_side.shape, f32),
            pltpu.VMEM(row_kind.shape, i32),
            pltpu.VMEM(cost.shape, f32),
            pltpu.VMEM(upper.shape, f32),
            pltpu.VMEM(primal_init.shape, f32),
            pltpu.VMEM(dual_init.shape, f32),
            pltpu.VMEM(dual_init.shape, f32),
            pltpu.VMEM((slots, LANES), i32),
            pltpu.VMEM((slots, LANES), i32),
            pltpu.VMEM((slots, LANES), i32),
            pltpu.VMEM((block // LANES, slots * 16, span), jnp.bfloat16),
            pltpu.VMEM((exchanges, span, LANES), f32),
            pltpu.VMEM((exchanges, span, LANES), f32),
            pltpu.SemaphoreType.DMA((9,)),
            pltpu.SemaphoreType.DMA((CHUNKS,)),
            pltpu.SemaphoreType.DMA((exchanges,)),
            pltpu.SemaphoreType.DMA((exchanges,)),
        ],
        compiler_params=pltpu.CompilerParams(
            collective_id=0, has_side_effects=True, vmem_limit_bytes=64 * 1024 * 1024
        ),
        name="pdhg",
    )
    return call(
        tile_rows,
        tile_cols,
        tile_count,
        tiles,
        right_side,
        row_kind,
        cost,
        upper,
        primal_init,
        dual_init,
    )


def solution(mesh):
    return jax.shard_map(
        per_device,
        mesh=mesh,
        in_specs=(
            P(("groups", "rows"), None, None),
            P(("groups", "rows")),
            P(("groups", "rows")),
            P(("groups", "rows")),
            P(("groups", "rows"), None),
            P(("groups", "rows"), None),
            P(("groups", "rows"), None),
            P(("groups", "rows"), None),
            P(("groups", "rows"), None),
            P(("groups", "rows"), None),
        ),
        out_specs=(P(("groups", "rows"), None), P(("groups", "rows"), None), P("groups", None)),
        check_vma=False,
    )
```

```python
import functools

import jax
import jax.numpy as jnp
from jax import lax
from jax.experimental import pallas as pl
from jax.experimental.pallas import tpu as pltpu
from jax.sharding import PartitionSpec as P

ITERS = 2
PRIMAL_STEP = 0.1
DUAL_STEP = 0.1
LANES = 128
MSG = 8
CHUNKS = 4
MESH = pl.DeviceIdType.MESH


def kernel(
    devices,
    rows_h,
    cols_h,
    count_h,
    tiles_h,
    right_h,
    kind_h,
    cost_h,
    upper_h,
    x_h,
    y_h,
    packed_out,
    rows_s,
    cols_s,
    count_s,
    tiles_v,
    flipped_v,
    right_v,
    kind_v,
    cost_v,
    upper_v,
    x_v,
    y_v,
    yb_v,
    peer_v,
    base_v,
    target_v,
    pick_v,
    send,
    recv,
    small_sem,
    tile_sem,
    send_sem,
    recv_sem,
):
    slots, block = tiles_v.shape[0], tiles_v.shape[1]
    row_count, col_count = right_v.shape[0], cost_v.shape[0]
    halves = block // LANES
    capacity = -(-slots // devices)
    per_vector = halves * capacity
    places = devices * capacity
    span = MSG * devices
    per_chunk = slots // CHUNKS
    me = lax.axis_index("rows")

    bits = devices.bit_length() - 1
    if devices != 1 << bits or per_vector * 2 > MSG or col_count > MSG:
        raise ValueError("unsupported sizes")

    def peer_of(step):
        peer = me
        for b in range(bits):
            one = 1 << b
            peer += ((step // one) % 2) * one * (1 - 2 * ((me // one) % 2))
        return peer

    def each_peer(do):
        if devices <= 16:
            for step in reversed(range(1, devices)):
                do(step)
        else:
            pl.loop(0, devices - 1)(lambda i: do(devices - 1 - i))

    barrier = pltpu.get_barrier_semaphore()

    def greet(step):
        pl.semaphore_signal(
            barrier, inc=1, device_id={"rows": peer_of(step)}, device_id_type=MESH
        )

    each_peer(greet)

    chunk_copies = []
    for c in range(CHUNKS):
        part = pl.ds(c * per_chunk, per_chunk)
        chunk_copies.append(
            pltpu.make_async_copy(tiles_h.at[part], tiles_v.at[part], tile_sem.at[c])
        )
    small_copies = []
    pairs = (
        (cols_h, cols_s),
        (count_h, count_s),
        (rows_h, rows_s),
        (y_h, y_v),
        (cost_h, cost_v),
        (upper_h, upper_v),
        (x_h, x_v),
        (right_h, right_v),
        (kind_h, kind_v),
    )
    for n, (src, dst) in enumerate(pairs):
        small_copies.append(pltpu.make_async_copy(src, dst, small_sem.at[n]))
    for copy in small_copies[:4]:
        copy.start()
    for copy in chunk_copies:
        copy.start()
    for copy in small_copies[4:]:
        copy.start()

    for copy in small_copies[:3]:
        copy.wait()

    lane = lax.broadcasted_iota(jnp.int32, (slots, LANES), 1)
    sub = lax.broadcasted_iota(jnp.int32, (slots, LANES), 0)
    lane1 = lax.broadcasted_iota(jnp.int32, (1, LANES), 1)
    peer_l = jnp.full((1, LANES), -1, jnp.int32)
    local_l = jnp.zeros((1, LANES), jnp.int32)
    for t in range(slots):
        col = cols_s[t]
        owner = col // col_count
        local = col - owner * col_count
        step = 0
        for b in range(bits):
            one = 1 << b
            step += ((owner // one + me // one) % 2) * one
        step = jnp.where(t < count_s[0], step, 16 * devices + t)
        peer_v[t : t + 1, :] = jnp.full((1, LANES), step, jnp.int32)
        peer_l = jnp.where(lane1 == t, step, peer_l)
        local_l = jnp.where(lane1 == t, local, local_l)
    peer_s = peer_v[...]
    same = peer_s == peer_l
    rank_s = jnp.sum(jnp.where(same & (lane < sub), 1.0, 0.0), axis=1, keepdims=True)
    rank_l = jnp.sum(jnp.where(same & (sub < lane), 1.0, 0.0), axis=0, keepdims=True)
    rank_s = rank_s.astype(jnp.int32)
    base_v[...] = peer_s * MSG + rank_s
    target_v[...] = peer_s + rank_s * devices
    target_l = peer_l + rank_l.astype(jnp.int32) * devices

    place = lax.broadcasted_iota(jnp.int32, (places, LANES), 0)
    found = (target_l == place) & (
        lax.broadcasted_iota(jnp.int32, (places, LANES), 1) < slots
    )
    col_of = jnp.sum(
        jnp.where(found, (local_l + 1).astype(jnp.float32), 0.0), axis=1, keepdims=True
    )
    col_of = jnp.broadcast_to(col_of - 1.0, (places, LANES))
    for s in range(capacity):
        send[0, pl.ds(per_vector + s, devices, stride=MSG), :] = col_of[
            s * devices : (s + 1) * devices
        ]

    wide_lane = lax.broadcasted_iota(jnp.int32, (16, span), 1)
    wide_sub = lax.broadcasted_iota(jnp.int32, (16, span), 0)
    vector_of = wide_sub // row_count
    row_of = jnp.where(vector_of < 2, wide_sub - vector_of * row_count, -1)
    wanted = wide_lane - vector_of * per_vector
    for t in range(slots):
        base = base_v[t : t + 1, :]
        if span > LANES:
            base = jnp.concatenate([base] * (span // LANES), axis=1)
        hit_row = row_of == rows_s[t]
        for h in range(halves):
            hit = hit_row & (wanted == base + h * capacity)
            pick_v[h, t * 16 : (t + 1) * 16, :] = jnp.where(hit, 1.0, 0.0).astype(
                jnp.bfloat16
            )

    place_wide = lax.broadcasted_iota(jnp.int32, (places, block), 0)

    def adjoint(first):
        total = jnp.zeros((places, block), jnp.float32)
        for c in range(CHUNKS):
            if first:
                chunk_copies[c].wait()
            parts = []
            for t in range(c * per_chunk, (c + 1) * per_chunk):
                row = yb_v[pl.ds(rows_s[t], 1), :]
                target = target_v[t : t + 1, :]
                target = jnp.concatenate([target] * halves, axis=1)
                parts.append(
                    jnp.where(target == place_wide, row, 0.0).astype(jnp.bfloat16)
                )
            left = jnp.concatenate(parts, axis=1)
            right = tiles_v[c * per_chunk : (c + 1) * per_chunk].reshape(
                per_chunk * block, block
            )
            total += jnp.dot(left, right, preferred_element_type=jnp.float32)
        return total

    message_row = lax.broadcasted_iota(jnp.int32, (span, LANES), 0) % MSG

    def forward(e):
        arrived = jnp.where(message_row < used[e], recv[e], 0.0).astype(jnp.bfloat16)
        picked = [
            jnp.dot(pick_v[h], arrived, preferred_element_type=jnp.float32).astype(
                jnp.bfloat16
            )
            for h in range(halves)
        ]
        total = jnp.zeros((16, block), jnp.float32)
        for c in range(CHUNKS):
            parts = []
            for t in range(c * per_chunk, (c + 1) * per_chunk):
                parts += [p[t * 16 : (t + 1) * 16] for p in picked]
            left = jnp.concatenate(parts, axis=1)
            right = flipped_v[c * per_chunk : (c + 1) * per_chunk].reshape(
                per_chunk * block, block
            )
            total += jnp.dot(left, right, preferred_element_type=jnp.float32)
        return total

    used = [per_vector] * (2 * ITERS + 2)
    used[0], used[1], used[-1] = per_vector + capacity, 2 * per_vector, 2 * ITERS

    def exchange(e):
        recv[e, 0 : used[e], :] = send[e, 0 : used[e], :]

        def go(step):
            pltpu.make_async_remote_copy(
                src_ref=send.at[e, pl.ds(pl.multiple_of(MSG * step, MSG), used[e])],
                dst_ref=recv.at[e, pl.ds(pl.multiple_of(MSG * step, MSG), used[e])],
                send_sem=send_sem.at[e],
                recv_sem=recv_sem.at[e],
                device_id={"rows": peer_of(step)},
                device_id_type=MESH,
            ).start()

        each_peer(go)

    def settle(buffer, sems, e):
        rest = buffer.at[e, pl.ds(MSG, (devices - 1) * used[e])]
        pltpu.make_async_copy(rest, rest, sems.at[e]).wait()

    def send_terms(e, terms):
        for s in range(capacity):
            for h in range(halves):
                send[e, pl.ds(h * capacity + s, devices, stride=MSG), :] = terms[
                    s * devices : (s + 1) * devices, h * LANES : (h + 1) * LANES
                ]
        exchange(e)

    sub8 = lax.broadcasted_iota(jnp.int32, (MSG, LANES), 0).astype(jnp.float32)

    def column_image(e):
        sums = [[jnp.zeros((MSG, LANES), jnp.float32) for _ in range(2)] for _ in range(halves)]
        count = 0
        for k in range(devices):
            for s in range(capacity):
                at = k * MSG + per_vector + s
                hit = recv[0, at : at + 1, :] == sub8
                for h in range(halves):
                    at = k * MSG + h * capacity + s
                    term = jnp.where(hit, recv[e, at : at + 1, :], 0.0)
                    sums[h][count % 2] += term
                count += 1
        whole = jnp.concatenate([a + b for a, b in sums], axis=1)
        return whole[:col_count]

    def put_vector(e, v, x):
        for s in range(capacity):
            asked = recv[0, pl.ds(per_vector + s, devices, stride=MSG), :]
            for h in range(halves):
                reply = jnp.zeros((devices, LANES), jnp.float32)
                for c in range(col_count):
                    reply = jnp.where(
                        asked == float(c), x[c : c + 1, h * LANES : (h + 1) * LANES], reply
                    )
                at = v * per_vector + h * capacity + s
                send[e, pl.ds(at, devices, stride=MSG), :] = reply

    def rounded(x):
        return x.astype(jnp.bfloat16).astype(jnp.float32)

    def lane_sum(x):
        x = jnp.sum(x * x, axis=0, keepdims=True)
        total = x[:, :LANES]
        for h in range(1, halves):
            total += x[:, h * LANES : (h + 1) * LANES]
        return total

    small_copies[3].wait()
    y = y_v[...]
    yb_v[...] = rounded(y)
    terms = adjoint(True)
    pl.semaphore_wait(barrier, devices - 1)
    send_terms(0, terms)
    for t in range(slots):
        flipped_v[t] = tiles_v[t].T
    for copy in small_copies[4:]:
        copy.wait()
    cost, upper, x = cost_v[...], upper_v[...], x_v[...]
    right = right_v[...]
    bounded = kind_v[...] == 1
    settle(recv, recv_sem, 0)
    put_vector(1, 1, rounded(x))
    col_image = column_image(0)
    last = 2 * ITERS + 1
    row_image = None
    for step in range(ITERS):
        out, back = 2 * step + 1, 2 * step + 2
        x_new = jnp.clip(x - PRIMAL_STEP * (cost - col_image), 0.0, upper)
        put_vector(out, 0, rounded(2.0 * x_new - x))
        exchange(out)
        settle(recv, recv_sem, out)
        images = forward(out)
        bar_image = images[:row_count]
        if step == 0:
            row_image = images[row_count : 2 * row_count]
        row_image = (bar_image + row_image) / 2.0
        y_new = y + DUAL_STEP * (right - bar_image)
        y_new = jnp.where(bounded, jnp.maximum(y_new, 0.0), y_new)
        yb_v[...] = rounded(y_new)
        send_terms(back, adjoint(False))
        violation = right - row_image
        violation = jnp.where(bounded, jnp.maximum(violation, 0.0), violation)
        send[last, 2 * step : 2 * step + 1, :] = lane_sum(violation)
        settle(recv, recv_sem, back)
        col_image = column_image(back)
        gap = x_new - jnp.clip(x_new - (cost - col_image), 0.0, upper)
        send[last, 2 * step + 1 : 2 * step + 2, :] = lane_sum(gap)
        x, y = x_new, y_new

    recv[last, 0 : used[last], :] = send[last, 0 : used[last], :]

    def tell(step):
        pltpu.make_async_remote_copy(
            src_ref=send.at[last, pl.ds(0, used[last])],
            dst_ref=recv.at[last, pl.ds(pl.multiple_of(MSG * step, MSG), used[last])],
            send_sem=send_sem.at[last],
            recv_sem=recv_sem.at[last],
            device_id={"rows": peer_of(step)},
            device_id_type=MESH,
        ).start()

    each_peer(tell)
    packed_out[0:col_count, :] = x
    packed_out[MSG : MSG + row_count, :] = y
    for e in range(last):
        settle(send, send_sem, e)
    settle(recv, recv_sem, last)
    sums = jnp.sum(recv[last].reshape(devices, MSG, LANES), axis=0)
    sums = jnp.sum(sums, axis=1, keepdims=True)
    kinds = lax.broadcasted_iota(jnp.int32, (MSG, 1), 0)
    row_scale = 1.0 / (row_count * devices * block)
    col_scale = 1.0 / (col_count * devices * block)
    scale = jnp.where(kinds % 2 == 0, row_scale, col_scale)
    roots = jnp.sqrt(sums * scale)
    side = lax.broadcasted_iota(jnp.int32, (1, LANES), 1)
    for step in range(ITERS):
        packed_out[2 * MSG + step : 2 * MSG + step + 1, :LANES] = jnp.where(
            side == 0, roots[2 * step : 2 * step + 1], roots[2 * step + 1 : 2 * step + 2]
        )
    settle(send, send_sem, last)


def unpack(packed, x_out, y_out, norm_out):
    x_out[...] = packed[: x_out.shape[0]]
    y_out[...] = packed[MSG : MSG + y_out.shape[0]]
    norm_out[...] = packed[2 * MSG : 2 * MSG + ITERS, :2]


def per_device(
    tiles,
    tile_rows,
    tile_cols,
    tile_count,
    right_side,
    row_kind,
    cost,
    upper,
    primal_init,
    dual_init,
):
    devices = lax.axis_size("rows")
    slots, block = tiles.shape[0], tiles.shape[1]
    span = MSG * devices
    exchanges = 2 * ITERS + 2
    f32, i32 = jnp.float32, jnp.int32
    anywhere = pl.BlockSpec(memory_space=pl.ANY)
    vmem = pl.BlockSpec(memory_space=pltpu.VMEM)
    places = devices * (-(-slots // devices))
    call = pl.pallas_call(
        functools.partial(kernel, devices),
        out_shape=jax.ShapeDtypeStruct((3 * MSG, block), f32),
        in_specs=[anywhere] * 10,
        out_specs=vmem,
        scratch_shapes=[
            pltpu.SMEM(tile_rows.shape, i32),
            pltpu.SMEM(tile_cols.shape, i32),
            pltpu.SMEM(tile_count.shape, i32),
            pltpu.VMEM(tiles.shape, tiles.dtype),
            pltpu.VMEM(tiles.shape, tiles.dtype),
            pltpu.VMEM(right_side.shape, f32),
            pltpu.VMEM(row_kind.shape, i32),
            pltpu.VMEM(cost.shape, f32),
            pltpu.VMEM(upper.shape, f32),
            pltpu.VMEM(primal_init.shape, f32),
            pltpu.VMEM(dual_init.shape, f32),
            pltpu.VMEM(dual_init.shape, f32),
            pltpu.VMEM((slots, LANES), i32),
            pltpu.VMEM((slots, LANES), i32),
            pltpu.VMEM((slots, LANES), i32),
            pltpu.VMEM((block // LANES, slots * 16, span), jnp.bfloat16),
            pltpu.VMEM((exchanges, span, LANES), f32),
            pltpu.VMEM((exchanges, span, LANES), f32),
            pltpu.SemaphoreType.DMA((9,)),
            pltpu.SemaphoreType.DMA((CHUNKS,)),
            pltpu.SemaphoreType.DMA((exchanges,)),
            pltpu.SemaphoreType.DMA((exchanges,)),
        ],
        compiler_params=pltpu.CompilerParams(
            collective_id=0, has_side_effects=True, vmem_limit_bytes=64 * 1024 * 1024
        ),
        name="pdhg",
    )
    packed = call(
        tile_rows,
        tile_cols,
        tile_count,
        tiles,
        right_side,
        row_kind,
        cost,
        upper,
        primal_init,
        dual_init,
    )
    return pl.pallas_call(
        unpack,
        out_shape=(
            jax.ShapeDtypeStruct(primal_init.shape, f32),
            jax.ShapeDtypeStruct(dual_init.shape, f32),
            jax.ShapeDtypeStruct((ITERS, 2), f32),
        ),
        in_specs=[vmem],
        out_specs=(vmem, vmem, vmem),
        name="unpack",
    )(packed)


def solution(mesh):
    return jax.shard_map(
        per_device,
        mesh=mesh,
        in_specs=(
            P(("groups", "rows"), None, None),
            P(("groups", "rows")),
            P(("groups", "rows")),
            P(("groups", "rows")),
            P(("groups", "rows"), None),
            P(("groups", "rows"), None),
            P(("groups", "rows"), None),
            P(("groups", "rows"), None),
            P(("groups", "rows"), None),
            P(("groups", "rows"), None),
        ),
        out_specs=(P(("groups", "rows"), None), P(("groups", "rows"), None), P("groups", None)),
        check_vma=False,
    )
```

```python
import functools

import jax
import jax.numpy as jnp
from jax import lax
from jax.experimental import pallas as pl
from jax.experimental.pallas import tpu as pltpu
from jax.sharding import PartitionSpec as P

ITERS = 2
PRIMAL_STEP = 0.1
DUAL_STEP = 0.1
LANES = 128
MSG = 8
CHUNKS = 4
MESH = pl.DeviceIdType.MESH


def kernel(
    devices,
    rows_h,
    cols_h,
    count_h,
    tiles_h,
    right_h,
    kind_h,
    cost_h,
    upper_h,
    x_h,
    y_h,
    packed_out,
    rows_s,
    cols_s,
    count_s,
    tiles_v,
    flipped_v,
    right_v,
    kind_v,
    cost_v,
    upper_v,
    x_v,
    y_v,
    yb_v,
    peer_v,
    base_v,
    target_v,
    pick_v,
    send,
    recv,
    small_sem,
    tile_sem,
    send_sem,
    recv_sem,
):
    slots, block = tiles_v.shape[0], tiles_v.shape[1]
    row_count, col_count = right_v.shape[0], cost_v.shape[0]
    halves = block // LANES
    capacity = -(-slots // devices)
    per_vector = halves * capacity
    places = devices * capacity
    span = MSG * devices
    per_chunk = slots // CHUNKS
    me = lax.axis_index("rows")

    bits = devices.bit_length() - 1
    if devices != 1 << bits or per_vector * 2 > MSG or col_count > MSG:
        raise ValueError("unsupported sizes")

    def peer_of(step):
        peer = me
        for b in range(bits):
            one = 1 << b
            peer += ((step // one) % 2) * one * (1 - 2 * ((me // one) % 2))
        return peer

    def each_peer(do):
        if devices <= 16:
            for step in reversed(range(1, devices)):
                do(step)
        else:
            pl.loop(0, devices - 1)(lambda i: do(devices - 1 - i))

    barrier = pltpu.get_barrier_semaphore()

    def greet(step):
        pl.semaphore_signal(
            barrier, inc=1, device_id={"rows": peer_of(step)}, device_id_type=MESH
        )

    each_peer(greet)

    chunk_copies = []
    for c in range(CHUNKS):
        part = pl.ds(c * per_chunk, per_chunk)
        chunk_copies.append(
            pltpu.make_async_copy(tiles_h.at[part], tiles_v.at[part], tile_sem.at[c])
        )
    small_copies = []
    pairs = (
        (cols_h, cols_s),
        (count_h, count_s),
        (rows_h, rows_s),
        (y_h, y_v),
        (cost_h, cost_v),
        (upper_h, upper_v),
        (x_h, x_v),
        (right_h, right_v),
        (kind_h, kind_v),
    )
    for n, (src, dst) in enumerate(pairs):
        small_copies.append(pltpu.make_async_copy(src, dst, small_sem.at[n]))
    for copy in small_copies[:4]:
        copy.start()
    for copy in chunk_copies:
        copy.start()
    for copy in small_copies[4:]:
        copy.start()

    for copy in small_copies[:3]:
        copy.wait()

    lane = lax.broadcasted_iota(jnp.int32, (slots, LANES), 1)
    sub = lax.broadcasted_iota(jnp.int32, (slots, LANES), 0)
    lane1 = lax.broadcasted_iota(jnp.int32, (1, LANES), 1)
    peer_l = jnp.full((1, LANES), -1, jnp.int32)
    local_l = jnp.zeros((1, LANES), jnp.int32)
    for t in range(slots):
        col = cols_s[t]
        owner = col // col_count
        local = col - owner * col_count
        step = 0
        for b in range(bits):
            one = 1 << b
            step += ((owner // one + me // one) % 2) * one
        step = jnp.where(t < count_s[0], step, 16 * devices + t)
        peer_v[t : t + 1, :] = jnp.full((1, LANES), step, jnp.int32)
        peer_l = jnp.where(lane1 == t, step, peer_l)
        local_l = jnp.where(lane1 == t, local, local_l)
    peer_s = peer_v[...]
    same = peer_s == peer_l
    rank_s = jnp.sum(jnp.where(same & (lane < sub), 1.0, 0.0), axis=1, keepdims=True)
    rank_l = jnp.sum(jnp.where(same & (sub < lane), 1.0, 0.0), axis=0, keepdims=True)
    rank_s = rank_s.astype(jnp.int32)
    base_v[...] = peer_s * MSG + rank_s
    target_v[...] = peer_s + rank_s * devices
    target_l = peer_l + rank_l.astype(jnp.int32) * devices

    place = lax.broadcasted_iota(jnp.int32, (places, LANES), 0)
    found = (target_l == place) & (
        lax.broadcasted_iota(jnp.int32, (places, LANES), 1) < slots
    )
    col_of = jnp.sum(
        jnp.where(found, (local_l + 1).astype(jnp.float32), 0.0), axis=1, keepdims=True
    )
    col_of = jnp.broadcast_to(col_of - 1.0, (places, LANES))
    for s in range(capacity):
        send[0, pl.ds(per_vector + s, devices, stride=MSG), :] = col_of[
            s * devices : (s + 1) * devices
        ]

    place_wide = lax.broadcasted_iota(jnp.int32, (places, block), 0)

    def adjoint(first):
        total = jnp.zeros((places, block), jnp.float32)
        for c in range(CHUNKS):
            if first:
                chunk_copies[c].wait()
            parts = []
            for t in range(c * per_chunk, (c + 1) * per_chunk):
                row = yb_v[pl.ds(rows_s[t], 1), :]
                target = target_v[t : t + 1, :]
                target = jnp.concatenate([target] * halves, axis=1)
                parts.append(
                    jnp.where(target == place_wide, row, 0.0).astype(jnp.bfloat16)
                )
            left = jnp.concatenate(parts, axis=1)
            right = tiles_v[c * per_chunk : (c + 1) * per_chunk].reshape(
                per_chunk * block, block
            )
            total += jnp.dot(left, right, preferred_element_type=jnp.float32)
        return total

    message_row = lax.broadcasted_iota(jnp.int32, (span, LANES), 0) % MSG

    def forward(e):
        arrived = jnp.where(message_row < used[e], recv[e], 0.0).astype(jnp.bfloat16)
        picked = [
            jnp.dot(pick_v[h], arrived, preferred_element_type=jnp.float32).astype(
                jnp.bfloat16
            )
            for h in range(halves)
        ]
        total = jnp.zeros((16, block), jnp.float32)
        for c in range(CHUNKS):
            parts = []
            for t in range(c * per_chunk, (c + 1) * per_chunk):
                parts += [p[t * 16 : (t + 1) * 16] for p in picked]
            left = jnp.concatenate(parts, axis=1)
            right = flipped_v[c * per_chunk : (c + 1) * per_chunk].reshape(
                per_chunk * block, block
            )
            total += jnp.dot(left, right, preferred_element_type=jnp.float32)
        return total

    used = [per_vector] * (2 * ITERS + 2)
    used[0], used[1], used[-1] = per_vector + capacity, 2 * per_vector, 2 * ITERS

    def exchange(e):
        recv[e, 0 : used[e], :] = send[e, 0 : used[e], :]

        def go(step):
            pltpu.make_async_remote_copy(
                src_ref=send.at[e, pl.ds(pl.multiple_of(MSG * step, MSG), used[e])],
                dst_ref=recv.at[e, pl.ds(pl.multiple_of(MSG * step, MSG), used[e])],
                send_sem=send_sem.at[e],
                recv_sem=recv_sem.at[e],
                device_id={"rows": peer_of(step)},
                device_id_type=MESH,
            ).start()

        each_peer(go)

    def settle(buffer, sems, e):
        rest = buffer.at[e, pl.ds(MSG, (devices - 1) * used[e])]
        pltpu.make_async_copy(rest, rest, sems.at[e]).wait()

    def send_terms(e, terms):
        for s in range(capacity):
            for h in range(halves):
                send[e, pl.ds(h * capacity + s, devices, stride=MSG), :] = terms[
                    s * devices : (s + 1) * devices, h * LANES : (h + 1) * LANES
                ]
        exchange(e)

    sub8 = lax.broadcasted_iota(jnp.int32, (MSG, LANES), 0).astype(jnp.float32)

    def column_image(e):
        sums = [[jnp.zeros((MSG, LANES), jnp.float32) for _ in range(2)] for _ in range(halves)]
        count = 0
        for k in range(devices):
            for s in range(capacity):
                at = k * MSG + per_vector + s
                hit = recv[0, at : at + 1, :] == sub8
                for h in range(halves):
                    at = k * MSG + h * capacity + s
                    term = jnp.where(hit, recv[e, at : at + 1, :], 0.0)
                    sums[h][count % 2] += term
                count += 1
        whole = jnp.concatenate([a + b for a, b in sums], axis=1)
        return whole[:col_count]

    def put_vector(e, v, x):
        for s in range(capacity):
            asked = recv[0, pl.ds(per_vector + s, devices, stride=MSG), :]
            for h in range(halves):
                reply = jnp.zeros((devices, LANES), jnp.float32)
                for c in range(col_count):
                    reply = jnp.where(
                        asked == float(c), x[c : c + 1, h * LANES : (h + 1) * LANES], reply
                    )
                at = v * per_vector + h * capacity + s
                send[e, pl.ds(at, devices, stride=MSG), :] = reply

    def rounded(x):
        return x.astype(jnp.bfloat16).astype(jnp.float32)

    def lane_sum(x):
        x = jnp.sum(x * x, axis=0, keepdims=True)
        total = x[:, :LANES]
        for h in range(1, halves):
            total += x[:, h * LANES : (h + 1) * LANES]
        return total

    small_copies[3].wait()
    y = y_v[...]
    yb_v[...] = rounded(y)
    terms = adjoint(True)
    pl.semaphore_wait(barrier, devices - 1)
    send_terms(0, terms)

    wide_lane = lax.broadcasted_iota(jnp.int32, (16, span), 1)
    wide_sub = lax.broadcasted_iota(jnp.int32, (16, span), 0)
    vector_of = wide_sub // row_count
    row_of = jnp.where(vector_of < 2, wide_sub - vector_of * row_count, -1)
    wanted = wide_lane - vector_of * per_vector
    for t in range(slots):
        base = base_v[t : t + 1, :]
        if span > LANES:
            base = jnp.concatenate([base] * (span // LANES), axis=1)
        hit_row = row_of == rows_s[t]
        for h in range(halves):
            hit = hit_row & (wanted == base + h * capacity)
            pick_v[h, t * 16 : (t + 1) * 16, :] = jnp.where(hit, 1.0, 0.0).astype(
                jnp.bfloat16
            )

    for t in range(slots):
        flipped_v[t] = tiles_v[t].T
    for copy in small_copies[4:]:
        copy.wait()
    cost, upper, x = cost_v[...], upper_v[...], x_v[...]
    right = right_v[...]
    bounded = kind_v[...] == 1
    settle(recv, recv_sem, 0)
    put_vector(1, 1, rounded(x))
    col_image = column_image(0)
    last = 2 * ITERS + 1
    row_image = None
    for step in range(ITERS):
        out, back = 2 * step + 1, 2 * step + 2
        x_new = jnp.clip(x - PRIMAL_STEP * (cost - col_image), 0.0, upper)
        put_vector(out, 0, rounded(2.0 * x_new - x))
        exchange(out)
        settle(recv, recv_sem, out)
        images = forward(out)
        bar_image = images[:row_count]
        if step == 0:
            row_image = images[row_count : 2 * row_count]
        row_image = (bar_image + row_image) / 2.0
        y_new = y + DUAL_STEP * (right - bar_image)
        y_new = jnp.where(bounded, jnp.maximum(y_new, 0.0), y_new)
        yb_v[...] = rounded(y_new)
        send_terms(back, adjoint(False))
        violation = right - row_image
        violation = jnp.where(bounded, jnp.maximum(violation, 0.0), violation)
        send[last, 2 * step : 2 * step + 1, :] = lane_sum(violation)
        settle(recv, recv_sem, back)
        col_image = column_image(back)
        gap = x_new - jnp.clip(x_new - (cost - col_image), 0.0, upper)
        send[last, 2 * step + 1 : 2 * step + 2, :] = lane_sum(gap)
        x, y = x_new, y_new

    recv[last, 0 : used[last], :] = send[last, 0 : used[last], :]

    def tell(step):
        pltpu.make_async_remote_copy(
            src_ref=send.at[last, pl.ds(0, used[last])],
            dst_ref=recv.at[last, pl.ds(pl.multiple_of(MSG * step, MSG), used[last])],
            send_sem=send_sem.at[last],
            recv_sem=recv_sem.at[last],
            device_id={"rows": peer_of(step)},
            device_id_type=MESH,
        ).start()

    each_peer(tell)
    packed_out[0:col_count, :] = x
    packed_out[MSG : MSG + row_count, :] = y
    for e in range(last):
        settle(send, send_sem, e)
    settle(recv, recv_sem, last)
    sums = jnp.sum(recv[last].reshape(devices, MSG, LANES), axis=0)
    sums = jnp.sum(sums, axis=1, keepdims=True)
    kinds = lax.broadcasted_iota(jnp.int32, (MSG, 1), 0)
    row_scale = 1.0 / (row_count * devices * block)
    col_scale = 1.0 / (col_count * devices * block)
    scale = jnp.where(kinds % 2 == 0, row_scale, col_scale)
    roots = jnp.sqrt(sums * scale)
    side = lax.broadcasted_iota(jnp.int32, (1, LANES), 1)
    for step in range(ITERS):
        packed_out[2 * MSG + step : 2 * MSG + step + 1, :LANES] = jnp.where(
            side == 0, roots[2 * step : 2 * step + 1], roots[2 * step + 1 : 2 * step + 2]
        )
    settle(send, send_sem, last)


def unpack(packed, x_out, y_out, norm_out):
    x_out[...] = packed[: x_out.shape[0]]
    y_out[...] = packed[MSG : MSG + y_out.shape[0]]
    norm_out[...] = packed[2 * MSG : 2 * MSG + ITERS, :2]


def per_device(
    tiles,
    tile_rows,
    tile_cols,
    tile_count,
    right_side,
    row_kind,
    cost,
    upper,
    primal_init,
    dual_init,
):
    devices = lax.axis_size("rows")
    slots, block = tiles.shape[0], tiles.shape[1]
    span = MSG * devices
    exchanges = 2 * ITERS + 2
    f32, i32 = jnp.float32, jnp.int32
    anywhere = pl.BlockSpec(memory_space=pl.ANY)
    vmem = pl.BlockSpec(memory_space=pltpu.VMEM)
    places = devices * (-(-slots // devices))
    call = pl.pallas_call(
        functools.partial(kernel, devices),
        out_shape=jax.ShapeDtypeStruct((3 * MSG, block), f32),
        in_specs=[anywhere] * 10,
        out_specs=vmem,
        scratch_shapes=[
            pltpu.SMEM(tile_rows.shape, i32),
            pltpu.SMEM(tile_cols.shape, i32),
            pltpu.SMEM(tile_count.shape, i32),
            pltpu.VMEM(tiles.shape, tiles.dtype),
            pltpu.VMEM(tiles.shape, tiles.dtype),
            pltpu.VMEM(right_side.shape, f32),
            pltpu.VMEM(row_kind.shape, i32),
            pltpu.VMEM(cost.shape, f32),
            pltpu.VMEM(upper.shape, f32),
            pltpu.VMEM(primal_init.shape, f32),
            pltpu.VMEM(dual_init.shape, f32),
            pltpu.VMEM(dual_init.shape, f32),
            pltpu.VMEM((slots, LANES), i32),
            pltpu.VMEM((slots, LANES), i32),
            pltpu.VMEM((slots, LANES), i32),
            pltpu.VMEM((block // LANES, slots * 16, span), jnp.bfloat16),
            pltpu.VMEM((exchanges, span, LANES), f32),
            pltpu.VMEM((exchanges, span, LANES), f32),
            pltpu.SemaphoreType.DMA((9,)),
            pltpu.SemaphoreType.DMA((CHUNKS,)),
            pltpu.SemaphoreType.DMA((exchanges,)),
            pltpu.SemaphoreType.DMA((exchanges,)),
        ],
        compiler_params=pltpu.CompilerParams(
            collective_id=0, has_side_effects=True, vmem_limit_bytes=64 * 1024 * 1024
        ),
        name="pdhg",
    )
    packed = call(
        tile_rows,
        tile_cols,
        tile_count,
        tiles,
        right_side,
        row_kind,
        cost,
        upper,
        primal_init,
        dual_init,
    )
    return pl.pallas_call(
        unpack,
        out_shape=(
            jax.ShapeDtypeStruct(primal_init.shape, f32),
            jax.ShapeDtypeStruct(dual_init.shape, f32),
            jax.ShapeDtypeStruct((ITERS, 2), f32),
        ),
        in_specs=[vmem],
        out_specs=(vmem, vmem, vmem),
        name="unpack",
    )(packed)


def solution(mesh):
    return jax.shard_map(
        per_device,
        mesh=mesh,
        in_specs=(
            P(("groups", "rows"), None, None),
            P(("groups", "rows")),
            P(("groups", "rows")),
            P(("groups", "rows")),
            P(("groups", "rows"), None),
            P(("groups", "rows"), None),
            P(("groups", "rows"), None),
            P(("groups", "rows"), None),
            P(("groups", "rows"), None),
            P(("groups", "rows"), None),
        ),
        out_specs=(P(("groups", "rows"), None), P(("groups", "rows"), None), P("groups", None)),
        check_vma=False,
    )
```
